32 devices in a mesh: parts: 2 (over y), frame: 8 (over z, x), freq: 2 (over core).
Axes of the slice: x: 2, y: 2, z: 4, core: 2. Of those that a mesh axis runs over, the one named last changes fastest.
Arguments:
- spectrogram: bfloat16 [2048, 8192], P('freq', ('parts', 'frame')), parts along dimension 1, may hold values from 0.049804688 to 5
- templates: float32 [4096, 512], P(('parts', 'freq'), 'frame'), parts along dimension 0, may hold values from 0.1 to 2
- activations: float32 [512, 8192], P(None, ('parts', 'frame')), parts along dimension 1, may hold values from 0.001 to 0.03
- score_mask: int32 [512, 64], P(None, ('parts', 'frame')), parts along dimension 1, may hold values from 0 to 1, as said below
Outputs:
- templates_new: float32 [4096, 512], P(('parts', 'freq'), 'frame'), parts along dimension 0
- activations_new: float32 [512, 8192], P(None, ('parts', 'frame')), parts along dimension 1
The draws below stay inside these ranges and needn't reach their ends.
There are 2 independent parts, one for each index of `parts`. The reference program is written for one: setup_inputs(seed, part) draws one part's arguments, and reference() takes and returns one part's arrays. A program takes and returns all parts, laid end to end along the dimension named above; each array names one. Nothing has to cross between parts.
Inputs may be any that keep to these rules, and one draw needn't show every extreme that they name: `score_mask`: 0/1 values.
All inputs are finite; a program needn't handle non-finite values.
Results may differ from the reference program's by a relative error of at most 0.00052.
Values may be sent and summed in bfloat16 or wider, within the bound.
A program may use at most 64 MiB of HBM per device.

```python
import math
import jax
import jax.numpy as jnp
from jax import lax

F = 2048
K = 512
BLOCK = 128
ITERS = 1
FRAMES = 4096
NBLOCKS = 32


def draw_score_mask(key, part):
    key = jax.random.fold_in(key, 7)
    first, second, third = jax.random.split(key, 3)
    note_level = jax.random.randint(first, (K, 1), 1, 9)
    block_level = jax.random.randint(second, (1, NBLOCKS), 1, 9)
    rolled = jax.random.randint(third, (K, NBLOCKS), 0, 64)
    return (rolled < note_level * block_level).astype(jnp.int32)


def block_scale(own_key, extent, pieces, low, top_value):
    def one(position, blocks):
        draws = jax.random.uniform(jax.random.fold_in(jax.random.fold_in(own_key, 6), position), (blocks,), jnp.float32, low / len(pieces), top_value / len(pieces))
        return jnp.repeat(jnp.exp(draws), extent[position] // blocks).reshape((-1,) + (1,) * (len(extent) - position - 1))

    loudness = one(*pieces[0])
    for cut in pieces[1:]:
        loudness = loudness * one(*cut)
    return loudness


def setup_inputs(seed: int = 0, part: int = 0) -> dict:
    keys = jax.random.split(jax.random.key(seed), 5)
    part_keys = jax.random.split(jax.random.fold_in(keys[4], part), 5)
    spectrogram = jnp.clip(jnp.exp(math.log(5.0) - 4.609084 * jax.random.uniform(part_keys[0], (F, FRAMES), jnp.float32) ** block_scale(part_keys[0], (F, FRAMES), ((0, 2), (1, 8)), -0.2, 0.2)), 0.049804688, 5.0).astype(jnp.bfloat16)
    templates = jnp.clip(jnp.exp(math.log(2.0) - 2.9957323 * jax.random.uniform(part_keys[1], (F, K), jnp.float32) ** block_scale(part_keys[1], (F, K), ((0, 2), (1, 8)), -0.2, 0.2)), 0.1, 2.0)
    activations = jnp.clip(jnp.exp(math.log(0.03) - 3.4011973 * jax.random.uniform(part_keys[2], (K, FRAMES), jnp.float32) ** block_scale(part_keys[2], (K, FRAMES), ((1, 8),), -0.2, 0.2)), 0.001, 0.03)
    score_mask = draw_score_mask(jax.random.fold_in(jax.random.fold_in(keys[4], part), 71), part)
    return {"spectrogram": spectrogram, "templates": templates, "activations": activations, "score_mask": score_mask}


def reference(spectrogram, templates, activations, score_mask):
    allowed = jnp.repeat(score_mask.astype(jnp.float32), BLOCK, axis=1)
    acts = activations * allowed
    temps = templates
    for step in range(ITERS):
        w_bf = temps.astype(jnp.bfloat16)
        h_bf = acts.astype(jnp.bfloat16)
        approx = jnp.dot(w_bf, h_bf, preferred_element_type=jnp.float32).astype(jnp.bfloat16)
        numer_h = jnp.dot(w_bf.T, spectrogram, preferred_element_type=jnp.float32)
        denom_h = jnp.dot(w_bf.T, approx, preferred_element_type=jnp.float32)
        acts = allowed * acts * numer_h / (denom_h + 1e-6)
        h_new = acts.astype(jnp.bfloat16)
        numer_w = jnp.dot(spectrogram, h_new.T, preferred_element_type=jnp.float32)
        gram = jnp.dot(h_new, h_new.T, preferred_element_type=jnp.float32)
        denom_w = jnp.dot(w_bf.astype(jnp.float32), gram, precision=lax.Precision.HIGHEST)
        temps = temps * numer_w / (denom_w + 1e-6)
    return temps, acts
```

```python
import jax
import jax.numpy as jnp
from jax import lax
from jax.experimental import pallas as pl
from jax.experimental.pallas import tpu as pltpu
from jax.sharding import PartitionSpec as P

BLOCK = 128
MESH = pl.DeviceIdType.MESH
NT = (((1,), (1,)), ((), ()))
F32 = jnp.float32
BF16 = jnp.bfloat16


def shards(spectrogram, templates, activations, score_mask):
    allowed = jnp.repeat(score_mask.astype(F32), BLOCK, axis=1)
    acts = activations * allowed
    temps = templates
    note_cols = temps.shape[1]
    h_bf = acts.astype(BF16)
    whole = lax.all_gather(temps.astype(BF16), "frame", axis=1, tiled=True)
    approx = jnp.dot(whole, h_bf, preferred_element_type=F32).astype(BF16)
    numer_h = jnp.einsum("fk,fn->kn", whole, spectrogram, preferred_element_type=F32)
    denom_h = jnp.einsum("fk,fn->kn", whole, approx, preferred_element_type=F32)
    numer_h, denom_h = lax.psum((numer_h, denom_h), "freq")
    acts = allowed * acts * numer_h / (denom_h + 1e-06)
    h_new = acts.astype(BF16)
    numer_w = lax.psum_scatter(
        jnp.einsum("kn,fn->kf", h_new, spectrogram, preferred_element_type=F32),
        "frame",
        scatter_dimension=0,
        tiled=True,
    ).T
    gram_local = jnp.einsum("kn,jn->kj", h_new, h_new, preferred_element_type=F32)
    gram = lax.psum(gram_local, "frame")
    own_cols = lax.dynamic_slice_in_dim(gram, lax.axis_index("frame") * note_cols, note_cols, 1)
    denom_w = jnp.dot(whole.astype(F32), own_cols, precision=lax.Precision.HIGHEST)
    temps = temps * numer_w / (denom_w + 1e-06)
    return (temps, acts)


def kernel(
    s_ref, t_ref, a_ref, m_ref, to_ref, ao_ref,
    wt, hbt, at, num, den, pnum, pden, hn, blk, xr, zr, gram,
    ws, wr, ns, nr, ds, dr, xs, xrs, zs, zrs, gs, gr,
):
    own, bins = t_ref.shape
    notes, frames = a_ref.shape
    half = notes // 2
    me = lax.axis_index("frame")
    c = lax.axis_index("freq")
    z, x = me // 2, me % 2
    across = z * 2 + 1 - x
    cp = 1 - c

    barrier = pltpu.get_barrier_semaphore()
    pl.semaphore_signal(barrier, inc=1, device_id={"frame": across}, device_id_type=MESH)
    pl.semaphore_signal(barrier, inc=1, device_id={"freq": cp}, device_id_type=MESH)

    @pl.when(z < 3)
    def _():
        pl.semaphore_signal(barrier, inc=1, device_id={"frame": me + 2}, device_id_type=MESH)

    @pl.when(z > 0)
    def _():
        pl.semaphore_signal(barrier, inc=1, device_id={"frame": me - 2}, device_id_type=MESH)

    wt[me] = t_ref[...].astype(BF16)
    pl.semaphore_wait(barrier, 2 + (z + 2) // 3 + (5 - z) // 3)

    def shard(idx, way):
        to = {0: across, 1: me + 2, 2: me - 2}[way]
        return pltpu.make_async_remote_copy(
            wt.at[idx], wt.at[idx], ws.at[way, idx], wr.at[idx],
            device_id={"frame": to}, device_id_type=MESH,
        )

    def numer_copy(idx):
        return pltpu.make_async_remote_copy(
            num.at[idx], pnum.at[idx], ns.at[idx], nr.at[idx],
            device_id={"freq": cp}, device_id_type=MESH,
        )

    def numer(idx):
        num[idx] = jnp.dot(wt[idx], s_ref[...], preferred_element_type=F32)
        numer_copy(idx).start()

    @pl.when(z < 3)
    def _():
        shard(me, 1).start()

    @pl.when(z > 0)
    def _():
        shard(me, 2).start()

    shard(me, 0).start()

    for b in range(frames // BLOCK):
        cols = slice(b * BLOCK, (b + 1) * BLOCK)
        held = a_ref[:, cols] * m_ref[:, b : b + 1].astype(F32)
        hbt[cols, :] = held.T.astype(BF16)
    numer(me)

    for s in range(1, 4):
        low, high = me - 2 * s, me + 2 * s

        @pl.when(z >= s)
        def _():
            shard(low, 0).wait_recv()

            @pl.when(z < 3)
            def _():
                shard(low, 1).start()

            shard(low, 0).start()

        @pl.when(z + s < 4)
        def _():
            shard(high, 0).wait_recv()

            @pl.when(z > 0)
            def _():
                shard(high, 2).start()

            shard(high, 0).start()

        @pl.when(z >= s)
        def _():
            numer(low)

        @pl.when(z + s < 4)
        def _():
            numer(high)

    def far(s):
        @pl.when(z >= s)
        def _():
            idx = across - 2 * s
            shard(idx, 0).wait_recv()
            numer(idx)

        if s:
            @pl.when(z + s < 4)
            def _():
                idx = across + 2 * s
                shard(idx, 0).wait_recv()
                numer(idx)

    for s in range(4):
        far(s)

    step = 256

    @pl.loop(0, bins // step)
    def _(j):
        cols = pl.ds(pl.multiple_of(j * step, step), step)
        w = wt[:, :, cols].reshape(notes, step)
        at[:, cols] = jnp.dot(hbt[...], w, preferred_element_type=F32).astype(BF16)

    def denom_copy(j):
        return pltpu.make_async_remote_copy(
            den.at[j], pden.at[j], ds.at[j], dr.at[j],
            device_id={"freq": cp}, device_id_type=MESH,
        )

    for j in range(2):
        w = wt[j * 4 : j * 4 + 4].reshape(half, bins)
        den[j] = lax.dot_general(w, at[...], NT, preferred_element_type=F32)
        denom_copy(j).start()

    for i in range(8):
        numer_copy(i).wait_recv()

    for j in range(2):
        denom_copy(j).wait_recv()
        rows = slice(j * half, (j + 1) * half)
        for b in range(frames // BLOCK):
            cols = slice(b * BLOCK, (b + 1) * BLOCK)
            allowed = m_ref[rows, b : b + 1].astype(F32)
            up = (num[j * 4 : j * 4 + 4, :, cols] + pnum[j * 4 : j * 4 + 4, :, cols]).reshape(half, BLOCK)
            under = den[j, :, cols] + pden[j, :, cols]
            new = allowed * (a_ref[rows, cols] * allowed) * up / (under + 1e-06)
            ao_ref[rows, cols] = new
            hn[rows, cols] = new.astype(BF16)

    order = [3 * (1 - z // 2), 0, 1 + z % 2, z]
    order[1] = 6 - order[0] - order[2] - z
    mine = pl.ds(pl.multiple_of(c * half, half), half)

    def partial(idx):
        h = hn[pl.ds(pl.multiple_of(idx * own, own), own), :]
        blk[idx, :, :bins] = lax.dot_general(h, s_ref[...], NT, preferred_element_type=F32)
        blk[idx, :, bins:] = lax.dot_general(h, hn[mine, :], NT, preferred_element_type=F32)

    def x_copy(d):
        return pltpu.make_async_remote_copy(
            blk.at[2 * d + 1 - x], xr.at[d], xs.at[d], xrs.at[d],
            device_id={"frame": across}, device_id_type=MESH,
        )

    def z_copy(d, way):
        to = me + 2 if way else me - 2
        return pltpu.make_async_remote_copy(
            blk.at[2 * d + x], zr.at[way, d], zs.at[d], zrs.at[way, d],
            device_id={"frame": to}, device_id_type=MESH,
        )

    for d in order:
        partial(2 * d + 1 - x)
        x_copy(d).start()

    for d in order[:3]:
        idx = 2 * d + x
        partial(idx)
        x_copy(d).wait_recv()
        blk[idx] += xr[d]

        @pl.when(d > z)
        def _():
            @pl.when(z > 0)
            def _():
                z_copy(d, 1).wait_recv()
                blk[idx] += zr[1, d]

            z_copy(d, 1).start()

        @pl.when(d < z)
        def _():
            @pl.when(z < 3)
            def _():
                z_copy(d, 0).wait_recv()
                blk[idx] += zr[0, d]

            z_copy(d, 0).start()

    partial(me)
    x_copy(z).wait_recv()
    blk[me] += xr[z]

    @pl.when(z > 0)
    def _():
        z_copy(z, 1).wait_recv()
        blk[me] += zr[1, z]

    @pl.when(z < 3)
    def _():
        z_copy(z, 0).wait_recv()
        blk[me] += zr[0, z]

    gram[c] = blk[me, :, bins:]
    share = pltpu.make_async_remote_copy(
        gram.at[c], gram.at[c], gs, gr, device_id={"freq": cp}, device_id_type=MESH
    )
    share.start()
    share.wait_recv()

    total = jnp.zeros((own, bins), F32)
    for j in range(2):
        g = gram[j]
        hi = g.astype(BF16)
        lo = (g - hi.astype(F32)).astype(BF16)
        w = wt[j * 4 : j * 4 + 4].reshape(half, bins)
        both = jnp.dot(jnp.concatenate([hi, lo], 0), w, preferred_element_type=F32)
        total = total + both[:own] + both[own:]
    to_ref[...] = t_ref[...] * blk[me, :, :bins] / (total + 1e-06)

    share.wait_send()
    for j in range(2):
        denom_copy(j).wait_send()
    for i in range(8):
        numer_copy(i).wait_send()
    for d in range(4):
        x_copy(d).wait_send()
        shard(2 * d + x, 0).wait_send()

        @pl.when(d != z)
        def _():
            z_copy(d, 0).wait_send()

        @pl.when(jnp.logical_and(d <= z, z < 3))
        def _():
            shard(2 * d + x, 1).wait_send()

        @pl.when(jnp.logical_and(d >= z, z > 0))
        def _():
            shard(2 * d + x, 2).wait_send()


def fused(spectrogram, templates, activations, score_mask):
    bins, own = templates.shape
    notes, frames = activations.shape
    half = notes // 2
    dma = pltpu.SemaphoreType.DMA
    wide = bins + half
    turned, acts = pl.pallas_call(
        kernel,
        out_shape=(
            jax.ShapeDtypeStruct((own, bins), F32),
            jax.ShapeDtypeStruct((notes, frames), F32),
        ),
        in_specs=[pl.BlockSpec(memory_space=pltpu.VMEM)] * 4,
        out_specs=[pl.BlockSpec(memory_space=pltpu.VMEM)] * 2,
        scratch_shapes=[
            pltpu.VMEM((8, own, bins), BF16),
            pltpu.VMEM((frames, notes), BF16),
            pltpu.VMEM((frames, bins), BF16),
            pltpu.VMEM((8, own, frames), F32),
            pltpu.VMEM((2, half, frames), F32),
            pltpu.VMEM((8, own, frames), F32),
            pltpu.VMEM((2, half, frames), F32),
            pltpu.VMEM((notes, frames), BF16),
            pltpu.VMEM((8, own, wide), F32),
            pltpu.VMEM((4, own, wide), F32),
            pltpu.VMEM((2, 4, own, wide), F32),
            pltpu.VMEM((2, own, half), F32),
            dma((3, 8)), dma((8,)), dma((8,)), dma((8,)), dma((2,)), dma((2,)),
            dma((4,)), dma((4,)), dma((4,)), dma((2, 4)), dma(()), dma(()),
        ],
        compiler_params=pltpu.CompilerParams(
            collective_id=0, has_side_effects=True, vmem_limit_bytes=48 * 1024 * 1024
        ),
    )(spectrogram, templates.T, activations, score_mask)
    return turned.T, acts


def solution(mesh):
    return jax.shard_map(
        fused if mesh.shape["frame"] == 8 else shards,
        mesh=mesh,
        in_specs=(
            P("freq", ("parts", "frame")),
            P(("parts", "freq"), "frame"),
            P(None, ("parts", "frame")),
            P(None, ("parts", "frame")),
        ),
        out_specs=(P(("parts", "freq"), "frame"), P(None, ("parts", "frame"))),
        check_vma=False,
    )
```

```python
import jax
import jax.numpy as jnp
from jax import lax
from jax.experimental import pallas as pl
from jax.experimental.pallas import tpu as pltpu
from jax.sharding import PartitionSpec as P

BLOCK = 128
MESH = pl.DeviceIdType.MESH
NT = (((1,), (1,)), ((), ()))
F32 = jnp.float32
BF16 = jnp.bfloat16


def shards(spectrogram, templates, activations, score_mask):
    allowed = jnp.repeat(score_mask.astype(F32), BLOCK, axis=1)
    acts = activations * allowed
    temps = templates
    note_cols = temps.shape[1]
    h_bf = acts.astype(BF16)
    whole = lax.all_gather(temps.astype(BF16), "frame", axis=1, tiled=True)
    approx = jnp.dot(whole, h_bf, preferred_element_type=F32).astype(BF16)
    numer_h = jnp.einsum("fk,fn->kn", whole, spectrogram, preferred_element_type=F32)
    denom_h = jnp.einsum("fk,fn->kn", whole, approx, preferred_element_type=F32)
    numer_h, denom_h = lax.psum((numer_h, denom_h), "freq")
    acts = allowed * acts * numer_h / (denom_h + 1e-06)
    h_new = acts.astype(BF16)
    numer_w = lax.psum_scatter(
        jnp.einsum("kn,fn->kf", h_new, spectrogram, preferred_element_type=F32),
        "frame",
        scatter_dimension=0,
        tiled=True,
    ).T
    gram_local = jnp.einsum("kn,jn->kj", h_new, h_new, preferred_element_type=F32)
    gram = lax.psum(gram_local, "frame")
    own_cols = lax.dynamic_slice_in_dim(gram, lax.axis_index("frame") * note_cols, note_cols, 1)
    denom_w = jnp.dot(whole.astype(F32), own_cols, precision=lax.Precision.HIGHEST)
    temps = temps * numer_w / (denom_w + 1e-06)
    return (temps, acts)


def kernel(
    s_hbm, t_ref, a_hbm, m_ref, to_ref, ao_ref,
    s_ref, a_ref, mt, wt, hbt, at, num, den, pnum, pden, hn, blk, out, xr, zr, gram,
    ls, ws, wr, ns, nr, ds, dr, xs, xrs, zs, zrs, gs, gr,
):
    own, bins = t_ref.shape
    notes, frames = a_ref.shape
    wide = bins + notes // 2
    half = notes // 2
    me = lax.axis_index("frame")
    c = lax.axis_index("freq")
    z, x = me // 2, me % 2
    across = z * 2 + 1 - x
    cp = 1 - c

    load_a = pltpu.make_async_copy(a_hbm, a_ref, ls.at[0])
    load_s = pltpu.make_async_copy(s_hbm, s_ref, ls.at[1])
    load_a.start()
    load_s.start()

    barrier = pltpu.get_barrier_semaphore()
    pl.semaphore_signal(barrier, inc=1, device_id={"frame": across}, device_id_type=MESH)
    pl.semaphore_signal(barrier, inc=1, device_id={"freq": cp}, device_id_type=MESH)

    @pl.when(z < 3)
    def _():
        pl.semaphore_signal(barrier, inc=1, device_id={"frame": me + 2}, device_id_type=MESH)

    @pl.when(z > 0)
    def _():
        pl.semaphore_signal(barrier, inc=1, device_id={"frame": me - 2}, device_id_type=MESH)

    wt[me] = t_ref[...].astype(BF16)
    pl.semaphore_wait(barrier, 2 + (z + 2) // 3 + (5 - z) // 3)

    def shard(idx, way):
        to = {0: across, 1: me + 2, 2: me - 2}[way]
        return pltpu.make_async_remote_copy(
            wt.at[idx], wt.at[idx], ws.at[way, idx], wr.at[idx],
            device_id={"frame": to}, device_id_type=MESH,
        )

    def numer_copy(idx):
        return pltpu.make_async_remote_copy(
            num.at[idx], pnum.at[idx], ns.at[idx], nr.at[idx],
            device_id={"freq": cp}, device_id_type=MESH,
        )

    def numer(idx):
        num[idx] = jnp.dot(wt[idx], s_ref[...], preferred_element_type=F32)
        numer_copy(idx).start()

    @pl.when(z < 3)
    def _():
        shard(me, 1).start()

    @pl.when(z > 0)
    def _():
        shard(me, 2).start()

    shard(me, 0).start()

    flags = m_ref[...].astype(F32)
    mt[...] = jnp.concatenate([flags, flags], 0).T
    load_a.wait()
    for b in range(frames // BLOCK):
        cols = slice(b * BLOCK, (b + 1) * BLOCK)
        held = a_ref[:, cols] * mt[:, b : b + 1]
        hbt[cols, :] = held.T.astype(BF16)
    load_s.wait()
    numer(me)

    for s in range(1, 4):
        low, high = me - 2 * s, me + 2 * s

        @pl.when(z >= s)
        def _():
            shard(low, 0).wait_recv()

            @pl.when(z < 3)
            def _():
                shard(low, 1).start()

            shard(low, 0).start()

        @pl.when(z + s < 4)
        def _():
            shard(high, 0).wait_recv()

            @pl.when(z > 0)
            def _():
                shard(high, 2).start()

            shard(high, 0).start()

        @pl.when(z >= s)
        def _():
            numer(low)

        @pl.when(z + s < 4)
        def _():
            numer(high)

    def far(s):
        @pl.when(z >= s)
        def _():
            idx = across - 2 * s
            shard(idx, 0).wait_recv()
            numer(idx)

        if s:
            @pl.when(z + s < 4)
            def _():
                idx = across + 2 * s
                shard(idx, 0).wait_recv()
                numer(idx)

    for s in range(4):
        far(s)

    step = 256

    @pl.loop(0, bins // step)
    def _(j):
        cols = pl.ds(pl.multiple_of(j * step, step), step)
        w = wt[:, :, cols].reshape(notes, step)
        at[:, cols] = jnp.dot(hbt[...], w, preferred_element_type=F32).astype(BF16)

    def denom_copy(j):
        return pltpu.make_async_remote_copy(
            den.at[j], pden.at[j], ds.at[j], dr.at[j],
            device_id={"freq": cp}, device_id_type=MESH,
        )

    for j in range(2):
        w = wt[j * 4 : j * 4 + 4].reshape(half, bins)
        den[j] = lax.dot_general(w, at[...], NT, preferred_element_type=F32)
        denom_copy(j).start()

    for i in range(8):
        numer_copy(i).wait_recv()

    for j in range(2):
        denom_copy(j).wait_recv()
        rows = slice(j * half, (j + 1) * half)
        for b in range(frames // BLOCK):
            cols = slice(b * BLOCK, (b + 1) * BLOCK)
            allowed = mt[rows, b : b + 1]
            up = (num[j * 4 : j * 4 + 4, :, cols] + pnum[j * 4 : j * 4 + 4, :, cols]).reshape(half, BLOCK)
            under = den[j, :, cols] + pden[j, :, cols]
            new = allowed * (a_ref[rows, cols] * allowed) * up / (under + 1e-06)
            ao_ref[rows, cols] = new
            hn[rows, cols] = new.astype(BF16)

    order = [3 * (1 - z // 2), 0, 1 + z % 2, z]
    order[1] = 6 - order[0] - order[2] - z
    mine = pl.ds(pl.multiple_of(c * half, half), half)

    def partial(idx):
        h = hn[pl.ds(pl.multiple_of(idx * own, own), own), :]
        blk[idx, :, :bins] = lax.dot_general(h, s_ref[...], NT, preferred_element_type=F32)
        blk[idx, :, bins:] = lax.dot_general(h, hn[mine, :], NT, preferred_element_type=F32)

    def encode(idx):
        powers = []
        for cols in (slice(0, bins), slice(bins, wide)):
            v = blk[idx, :, cols]
            top = jnp.max(v, axis=1, keepdims=True)
            power = jnp.ceil(jnp.log2(jnp.maximum(top, 1e-30)))
            q = jnp.minimum(jnp.round(v * jnp.exp2(16.0 - power)) - 32768.0, 32767.0)
            out[idx, :, cols] = q.astype(jnp.int32).astype(jnp.int16)
            powers.append(jnp.broadcast_to(power, (own, BLOCK)))
        lane = lax.broadcasted_iota(jnp.int32, (own, BLOCK), 1)
        power = jnp.where(lane < BLOCK // 2, powers[0], powers[1])
        out[idx, :, wide:] = power.astype(jnp.int32).astype(jnp.int16)

    def add(idx, ref):
        scale = jnp.exp2(ref[:, wide:].astype(jnp.int32).astype(F32) - 16.0)
        for cols, col in ((slice(0, bins), 0), (slice(bins, wide), BLOCK - 1)):
            v = ref[:, cols].astype(jnp.int32).astype(F32) + 32768.0
            blk[idx, :, cols] += v * scale[:, col : col + 1]

    def x_copy(d):
        return pltpu.make_async_remote_copy(
            out.at[2 * d + 1 - x], xr.at[d], xs.at[d], xrs.at[d],
            device_id={"frame": across}, device_id_type=MESH,
        )

    def z_copy(d, way):
        to = me + 2 if way else me - 2
        return pltpu.make_async_remote_copy(
            out.at[2 * d + x], zr.at[way, d], zs.at[d], zrs.at[way, d],
            device_id={"frame": to}, device_id_type=MESH,
        )

    for d in order:
        partial(2 * d + 1 - x)
        encode(2 * d + 1 - x)
        x_copy(d).start()

    for d in order[:3]:
        idx = 2 * d + x
        partial(idx)
        x_copy(d).wait_recv()
        add(idx, xr.at[d])

        @pl.when(d > z)
        def _():
            @pl.when(z > 0)
            def _():
                z_copy(d, 1).wait_recv()
                add(idx, zr.at[1, d])

            encode(idx)
            z_copy(d, 1).start()

        @pl.when(d < z)
        def _():
            @pl.when(z < 3)
            def _():
                z_copy(d, 0).wait_recv()
                add(idx, zr.at[0, d])

            encode(idx)
            z_copy(d, 0).start()

    partial(me)
    x_copy(z).wait_recv()
    add(me, xr.at[z])

    @pl.when(z > 0)
    def _():
        z_copy(z, 1).wait_recv()
        add(me, zr.at[1, z])

    @pl.when(z < 3)
    def _():
        z_copy(z, 0).wait_recv()
        add(me, zr.at[0, z])

    gram[c] = blk[me, :, bins:]
    share = pltpu.make_async_remote_copy(
        gram.at[c], gram.at[c], gs, gr, device_id={"freq": cp}, device_id_type=MESH
    )
    share.start()
    share.wait_recv()

    total = jnp.zeros((own, bins), F32)
    for j in range(2):
        g = gram[j]
        hi = g.astype(BF16)
        lo = (g - hi.astype(F32)).astype(BF16)
        w = wt[j * 4 : j * 4 + 4].reshape(half, bins)
        both = jnp.dot(jnp.concatenate([hi, lo], 0), w, preferred_element_type=F32)
        total = total + both[:own] + both[own:]
    to_ref[...] = t_ref[...] * blk[me, :, :bins] / (total + 1e-06)

    share.wait_send()
    for j in range(2):
        denom_copy(j).wait_send()
    for i in range(8):
        numer_copy(i).wait_send()
    for d in range(4):
        x_copy(d).wait_send()
        shard(2 * d + x, 0).wait_send()

        @pl.when(d != z)
        def _():
            z_copy(d, 0).wait_send()

        @pl.when(jnp.logical_and(d <= z, z < 3))
        def _():
            shard(2 * d + x, 1).wait_send()

        @pl.when(jnp.logical_and(d >= z, z > 0))
        def _():
            shard(2 * d + x, 2).wait_send()


def fused(spectrogram, templates, activations, score_mask):
    bins, own = templates.shape
    notes, frames = activations.shape
    half = notes // 2
    dma = pltpu.SemaphoreType.DMA
    wide = bins + half
    turned, acts = pl.pallas_call(
        kernel,
        out_shape=(
            jax.ShapeDtypeStruct((own, bins), F32),
            jax.ShapeDtypeStruct((notes, frames), F32),
        ),
        in_specs=[pl.BlockSpec(memory_space=m) for m in (pltpu.HBM, pltpu.VMEM, pltpu.HBM, pltpu.VMEM)],
        out_specs=[pl.BlockSpec(memory_space=pltpu.VMEM)] * 2,
        scratch_shapes=[
            pltpu.VMEM((bins, frames), BF16),
            pltpu.VMEM((notes, frames), F32),
            pltpu.VMEM((notes, 8), F32),
            pltpu.VMEM((8, own, bins), BF16),
            pltpu.VMEM((frames, notes), BF16),
            pltpu.VMEM((frames, bins), BF16),
            pltpu.VMEM((8, own, frames), F32),
            pltpu.VMEM((2, half, frames), F32),
            pltpu.VMEM((8, own, frames), F32),
            pltpu.VMEM((2, half, frames), F32),
            pltpu.VMEM((notes, frames), BF16),
            pltpu.VMEM((8, own, wide), F32),
            pltpu.VMEM((8, own, wide + BLOCK), jnp.int16),
            pltpu.VMEM((4, own, wide + BLOCK), jnp.int16),
            pltpu.VMEM((2, 4, own, wide + BLOCK), jnp.int16),
            pltpu.VMEM((2, own, half), F32),
            dma((2,)), dma((3, 8)), dma((8,)), dma((8,)), dma((8,)), dma((2,)), dma((2,)),
            dma((4,)), dma((4,)), dma((4,)), dma((2, 4)), dma(()), dma(()),
        ],
        compiler_params=pltpu.CompilerParams(
            collective_id=0, has_side_effects=True, vmem_limit_bytes=48 * 1024 * 1024
        ),
    )(spectrogram, templates.T, activations, score_mask.T)
    return turned.T, acts


def solution(mesh):
    return jax.shard_map(
        fused if mesh.shape["frame"] == 8 else shards,
        mesh=mesh,
        in_specs=(
            P("freq", ("parts", "frame")),
            P(("parts", "freq"), "frame"),
            P(None, ("parts", "frame")),
            P(None, ("parts", "frame")),
        ),
        out_specs=(P(("parts", "freq"), "frame"), P(None, ("parts", "frame"))),
        check_vma=False,
    )
```

```python
import jax
import jax.numpy as jnp
from jax import lax
from jax.experimental import pallas as pl
from jax.experimental.pallas import tpu as pltpu
from jax.sharding import PartitionSpec as P

BLOCK = 128
MESH = pl.DeviceIdType.MESH
NT = (((1,), (1,)), ((), ()))
F32 = jnp.float32
BF16 = jnp.bfloat16


def shards(spectrogram, templates, activations, score_mask):
    allowed = jnp.repeat(score_mask.astype(F32), BLOCK, axis=1)
    acts = activations * allowed
    temps = templates
    note_cols = temps.shape[1]
    h_bf = acts.astype(BF16)
    whole = lax.all_gather(temps.astype(BF16), "frame", axis=1, tiled=True)
    approx = jnp.dot(whole, h_bf, preferred_element_type=F32).astype(BF16)
    numer_h = jnp.einsum("fk,fn->kn", whole, spectrogram, preferred_element_type=F32)
    denom_h = jnp.einsum("fk,fn->kn", whole, approx, preferred_element_type=F32)
    numer_h, denom_h = lax.psum((numer_h, denom_h), "freq")
    acts = allowed * acts * numer_h / (denom_h + 1e-06)
    h_new = acts.astype(BF16)
    numer_w = lax.psum_scatter(
        jnp.einsum("kn,fn->kf", h_new, spectrogram, preferred_element_type=F32),
        "frame",
        scatter_dimension=0,
        tiled=True,
    ).T
    gram_local = jnp.einsum("kn,jn->kj", h_new, h_new, preferred_element_type=F32)
    gram = lax.psum(gram_local, "frame")
    own_cols = lax.dynamic_slice_in_dim(gram, lax.axis_index("frame") * note_cols, note_cols, 1)
    denom_w = jnp.dot(whole.astype(F32), own_cols, precision=lax.Precision.HIGHEST)
    temps = temps * numer_w / (denom_w + 1e-06)
    return (temps, acts)


def kernel(
    s_hbm, t_hbm, a_hbm, m_hbm, to_ref, ao_hbm,
    s_ref, t_ref, a_ref, m_ref, ao_ref, mt, wt, hbt, at, num, den, pnum, pden, hn, blk, out, xr, zr, gram,
    ls, ws, wr, ns, nr, ds, dr, xs, xrs, zs, zrs, gs, gr,
):
    own, bins = t_ref.shape
    notes, frames = a_ref.shape
    wide = bins + notes // 2
    half = notes // 2
    me = lax.axis_index("frame")
    c = lax.axis_index("freq")
    z, x = me // 2, me % 2
    across = z * 2 + 1 - x
    cp = 1 - c

    load_a = pltpu.make_async_copy(a_hbm, a_ref, ls.at[0])
    load_s = pltpu.make_async_copy(s_hbm, s_ref, ls.at[1])
    load_t = pltpu.make_async_copy(t_hbm, t_ref, ls.at[2])
    load_m = pltpu.make_async_copy(m_hbm, m_ref, ls.at[3])
    for load in (load_t, load_m, load_a, load_s):
        load.start()

    barrier = pltpu.get_barrier_semaphore()
    pl.semaphore_signal(barrier, inc=1, device_id={"frame": across}, device_id_type=MESH)
    pl.semaphore_signal(barrier, inc=1, device_id={"freq": cp}, device_id_type=MESH)

    @pl.when(z < 3)
    def _():
        pl.semaphore_signal(barrier, inc=1, device_id={"frame": me + 2}, device_id_type=MESH)

    @pl.when(z > 0)
    def _():
        pl.semaphore_signal(barrier, inc=1, device_id={"frame": me - 2}, device_id_type=MESH)

    load_t.wait()
    wt[me] = t_ref[...].astype(BF16)
    pl.semaphore_wait(barrier, 2 + (z + 2) // 3 + (5 - z) // 3)

    def shard(idx, way, part):
        to = {0: across, 1: me + 2, 2: me - 2}[way]
        rows = pl.ds(part * (own // 2), own // 2)
        return pltpu.make_async_remote_copy(
            wt.at[idx, rows], wt.at[idx, rows], ws.at[way, idx, part], wr.at[idx, part],
            device_id={"frame": to}, device_id_type=MESH,
        )

    def send(idx, way):
        for part in range(2):
            shard(idx, way, part).start()

    def arrive(idx):
        for part in range(2):
            shard(idx, 0, part).wait_recv()

    first, last = 1 - x, 7 - x

    def numer_copy(idx):
        return pltpu.make_async_remote_copy(
            num.at[idx], pnum.at[idx], ns.at[idx], nr.at[idx],
            device_id={"freq": cp}, device_id_type=MESH,
        )

    def numer(idx):
        num[idx] = jnp.dot(wt[idx], s_ref[...], preferred_element_type=F32)
        numer_copy(idx).start()

    @pl.when(z < 3)
    def _():
        send(me, 1)

    @pl.when(z > 0)
    def _():
        send(me, 2)

    send(me, 0)

    load_m.wait()
    flags = m_ref[...].astype(F32)
    mt[...] = jnp.concatenate([flags, flags], 0).T
    load_a.wait()
    for b in range(frames // BLOCK):
        cols = slice(b * BLOCK, (b + 1) * BLOCK)
        held = a_ref[:, cols] * mt[:, b : b + 1]
        hbt[cols, :] = held.T.astype(BF16)
    load_s.wait()

    def forward(s):
        low, high = me - 2 * s, me + 2 * s

        @pl.when(z >= s)
        def _():
            arrive(low)

            @pl.when(z < 3)
            def _():
                send(low, 1)

            shard(low, 0, 0).start()

            @pl.when(z > s)
            def _():
                shard(low, 0, 1).start()

        @pl.when(z + s < 4)
        def _():
            arrive(high)

            @pl.when(z > 0)
            def _():
                send(high, 2)

            shard(high, 0, 0).start()

            @pl.when(z + s < 3)
            def _():
                shard(high, 0, 1).start()

    def near(s):
        @pl.when(z >= s)
        def _():
            numer(me - 2 * s)

        @pl.when(z + s < 4)
        def _():
            numer(me + 2 * s)

    def far(s):
        @pl.when(z >= s)
        def _():
            idx = across - 2 * s
            shard(idx, 0, 0).wait_recv()

            @pl.when(jnp.logical_or(z > s, z == 3))
            def _():
                shard(idx, 0, 1).wait_recv()

            numer(idx)

        @pl.when(z + s < 4)
        def _():
            idx = across + 2 * s
            shard(idx, 0, 0).wait_recv()

            @pl.when(jnp.logical_or(z + s < 3, z == 0))
            def _():
                shard(idx, 0, 1).wait_recv()

            numer(idx)

    def along(up, down):
        @pl.when(z == up)
        def _():
            shard(first, 0, 1).wait_recv()
            shard(first, 1, 1).start()

        @pl.when(z == down)
        def _():
            shard(last, 0, 1).wait_recv()
            shard(last, 2, 1).start()

    forward(1)
    arrive(across)

    @pl.when(z == 0)
    def _():
        shard(first, 1, 1).start()

    @pl.when(z == 3)
    def _():
        shard(last, 2, 1).start()

    numer(me)
    numer(across)
    forward(2)
    near(1)
    along(1, 2)
    far(1)
    forward(3)
    near(2)
    along(2, 1)
    near(3)
    far(2)
    far(3)

    def store(j):
        rows = pl.ds(j * half, half)
        return pltpu.make_async_copy(ao_ref.at[rows], ao_hbm.at[rows], ls.at[4 + j])

    step = 256

    @pl.loop(0, bins // step)
    def _(j):
        cols = pl.ds(pl.multiple_of(j * step, step), step)
        w = wt[:, :, cols].reshape(notes, step)
        at[:, cols] = jnp.dot(hbt[...], w, preferred_element_type=F32).astype(BF16)

    def denom_copy(j):
        return pltpu.make_async_remote_copy(
            den.at[j], pden.at[j], ds.at[j], dr.at[j],
            device_id={"freq": cp}, device_id_type=MESH,
        )

    for j in range(2):
        w = wt[j * 4 : j * 4 + 4].reshape(half, bins)
        den[j] = lax.dot_general(w, at[...], NT, preferred_element_type=F32)
        denom_copy(j).start()

    for i in range(8):
        numer_copy(i).wait_recv()

    for j in range(2):
        denom_copy(j).wait_recv()
        rows = slice(j * half, (j + 1) * half)
        for b in range(frames // BLOCK):
            cols = slice(b * BLOCK, (b + 1) * BLOCK)
            allowed = mt[rows, b : b + 1]
            up = (num[j * 4 : j * 4 + 4, :, cols] + pnum[j * 4 : j * 4 + 4, :, cols]).reshape(half, BLOCK)
            under = den[j, :, cols] + pden[j, :, cols]
            new = allowed * (a_ref[rows, cols] * allowed) * up / (under + 1e-06)
            ao_ref[rows, cols] = new
            hn[rows, cols] = new.astype(BF16)
        store(j).start()

    order = [3 * (1 - z // 2), 0, 1 + z % 2, z]
    order[1] = 6 - order[0] - order[2] - z
    mine = pl.ds(pl.multiple_of(c * half, half), half)

    def partial(idx):
        h = hn[pl.ds(pl.multiple_of(idx * own, own), own), :]
        blk[idx, :, :bins] = lax.dot_general(h, s_ref[...], NT, preferred_element_type=F32)
        blk[idx, :, bins:] = lax.dot_general(h, hn[mine, :], NT, preferred_element_type=F32)

    def encode(idx):
        powers = []
        for cols in (slice(0, bins), slice(bins, wide)):
            v = blk[idx, :, cols]
            top = jnp.max(v, axis=1, keepdims=True)
            power = jnp.ceil(jnp.log2(jnp.maximum(top, 1e-30)))
            q = jnp.minimum(jnp.round(v * jnp.exp2(16.0 - power)) - 32768.0, 32767.0)
            out[idx, :, cols] = q.astype(jnp.int32).astype(jnp.int16)
            powers.append(jnp.broadcast_to(power, (own, BLOCK)))
        lane = lax.broadcasted_iota(jnp.int32, (own, BLOCK), 1)
        power = jnp.where(lane < BLOCK // 2, powers[0], powers[1])
        out[idx, :, wide:] = power.astype(jnp.int32).astype(jnp.int16)

    def add(idx, ref):
        scale = jnp.exp2(ref[:, wide:].astype(jnp.int32).astype(F32) - 16.0)
        for cols, col in ((slice(0, bins), 0), (slice(bins, wide), BLOCK - 1)):
            v = ref[:, cols].astype(jnp.int32).astype(F32) + 32768.0
            blk[idx, :, cols] += v * scale[:, col : col + 1]

    def x_copy(d):
        return pltpu.make_async_remote_copy(
            out.at[2 * d + 1 - x], xr.at[d], xs.at[d], xrs.at[d],
            device_id={"frame": across}, device_id_type=MESH,
        )

    def z_copy(d, way):
        to = me + 2 if way else me - 2
        return pltpu.make_async_remote_copy(
            out.at[2 * d + x], zr.at[way, d], zs.at[d], zrs.at[way, d],
            device_id={"frame": to}, device_id_type=MESH,
        )

    for d in order:
        partial(2 * d + 1 - x)
        encode(2 * d + 1 - x)
        x_copy(d).start()

    for d in order[:3]:
        idx = 2 * d + x
        partial(idx)
        x_copy(d).wait_recv()
        add(idx, xr.at[d])

        @pl.when(d > z)
        def _():
            @pl.when(z > 0)
            def _():
                z_copy(d, 1).wait_recv()
                add(idx, zr.at[1, d])

            encode(idx)
            z_copy(d, 1).start()

        @pl.when(d < z)
        def _():
            @pl.when(z < 3)
            def _():
                z_copy(d, 0).wait_recv()
                add(idx, zr.at[0, d])

            encode(idx)
            z_copy(d, 0).start()

    partial(me)
    x_copy(z).wait_recv()
    add(me, xr.at[z])

    @pl.when(z > 0)
    def _():
        z_copy(z, 1).wait_recv()
        add(me, zr.at[1, z])

    @pl.when(z < 3)
    def _():
        z_copy(z, 0).wait_recv()
        add(me, zr.at[0, z])

    gram[c] = blk[me, :, bins:]
    share = pltpu.make_async_remote_copy(
        gram.at[c], gram.at[c], gs, gr, device_id={"freq": cp}, device_id_type=MESH
    )
    share.start()
    share.wait_recv()

    total = jnp.zeros((own, bins), F32)
    for j in range(2):
        g = gram[j]
        hi = g.astype(BF16)
        lo = (g - hi.astype(F32)).astype(BF16)
        w = wt[j * 4 : j * 4 + 4].reshape(half, bins)
        both = jnp.dot(jnp.concatenate([hi, lo], 0), w, preferred_element_type=F32)
        total = total + both[:own] + both[own:]
    to_ref[...] = t_ref[...] * blk[me, :, :bins] / (total + 1e-06)

    share.wait_send()
    for j in range(2):
        denom_copy(j).wait_send()
        store(j).wait()
    for i in range(8):
        numer_copy(i).wait_send()
    for d in range(4):
        x_copy(d).wait_send()
        shard(2 * d + x, 0, 0).wait_send()

        @pl.when(d == z if d in (0, 3) else d >= 0 * z)
        def _():
            shard(2 * d + x, 0, 1).wait_send()

        @pl.when(d != z)
        def _():
            z_copy(d, 0).wait_send()

        @pl.when(jnp.logical_and(d <= z, z < 3))
        def _():
            for part in range(2):
                shard(2 * d + x, 1, part).wait_send()

        @pl.when(jnp.logical_and(d >= z, z > 0))
        def _():
            for part in range(2):
                shard(2 * d + x, 2, part).wait_send()

    @pl.when(z < 3)
    def _():
        shard(first, 1, 1).wait_send()

    @pl.when(z > 0)
    def _():
        shard(last, 2, 1).wait_send()


def fused(spectrogram, templates, activations, score_mask):
    bins, own = templates.shape
    notes, frames = activations.shape
    half = notes // 2
    dma = pltpu.SemaphoreType.DMA
    wide = bins + half
    turned, acts = pl.pallas_call(
        kernel,
        out_shape=(
            jax.ShapeDtypeStruct((own, bins), F32),
            jax.ShapeDtypeStruct((notes, frames), F32),
        ),
        in_specs=[pl.BlockSpec(memory_space=pltpu.HBM)] * 4,
        out_specs=[pl.BlockSpec(memory_space=m) for m in (pltpu.VMEM, pltpu.HBM)],
        scratch_shapes=[
            pltpu.VMEM((bins, frames), BF16),
            pltpu.VMEM((own, bins), F32),
            pltpu.VMEM((notes, frames), F32),
            pltpu.VMEM((frames // BLOCK, notes), jnp.int32),
            pltpu.VMEM((notes, frames), F32),
            pltpu.VMEM((notes, 8), F32),
            pltpu.VMEM((8, own, bins), BF16),
            pltpu.VMEM((frames, notes), BF16),
            pltpu.VMEM((frames, bins), BF16),
            pltpu.VMEM((8, own, frames), F32),
            pltpu.VMEM((2, half, frames), F32),
            pltpu.VMEM((8, own, frames), F32),
            pltpu.VMEM((2, half, frames), F32),
            pltpu.VMEM((notes, frames), BF16),
            pltpu.VMEM((8, own, wide), F32),
            pltpu.VMEM((8, own, wide + BLOCK), jnp.int16),
            pltpu.VMEM((4, own, wide + BLOCK), jnp.int16),
            pltpu.VMEM((2, 4, own, wide + BLOCK), jnp.int16),
            pltpu.VMEM((2, own, half), F32),
            dma((6,)), dma((3, 8, 2)), dma((8, 2)), dma((8,)), dma((8,)), dma((2,)), dma((2,)),
            dma((4,)), dma((4,)), dma((4,)), dma((2, 4)), dma(()), dma(()),
        ],
        compiler_params=pltpu.CompilerParams(
            collective_id=0, has_side_effects=True, vmem_limit_bytes=60 * 1024 * 1024
        ),
    )(spectrogram, templates.T, activations, score_mask.T)
    return turned.T, acts


def solution(mesh):
    return jax.shard_map(
        fused if mesh.shape["frame"] == 8 else shards,
        mesh=mesh,
        in_specs=(
            P("freq", ("parts", "frame")),
            P(("parts", "freq"), "frame"),
            P(None, ("parts", "frame")),
            P(None, ("parts", "frame")),
        ),
        out_specs=(P(("parts", "freq"), "frame"), P(None, ("parts", "frame"))),
        check_vma=False,
    )
```

```python
import jax
import jax.numpy as jnp
from jax import lax
from jax.experimental import pallas as pl
from jax.experimental.pallas import tpu as pltpu
from jax.sharding import PartitionSpec as P

BLOCK = 128
MESH = pl.DeviceIdType.MESH
NT = (((1,), (1,)), ((), ()))
F32 = jnp.float32
BF16 = jnp.bfloat16


def shards(spectrogram, templates, activations, score_mask):
    allowed = jnp.repeat(score_mask.astype(F32), BLOCK, axis=1)
    acts = activations * allowed
    temps = templates
    note_cols = temps.shape[1]
    h_bf = acts.astype(BF16)
    whole = lax.all_gather(temps.astype(BF16), "frame", axis=1, tiled=True)
    approx = jnp.dot(whole, h_bf, preferred_element_type=F32).astype(BF16)
    numer_h = jnp.einsum("fk,fn->kn", whole, spectrogram, preferred_element_type=F32)
    denom_h = jnp.einsum("fk,fn->kn", whole, approx, preferred_element_type=F32)
    numer_h, denom_h = lax.psum((numer_h, denom_h), "freq")
    acts = allowed * acts * numer_h / (denom_h + 1e-06)
    h_new = acts.astype(BF16)
    numer_w = lax.psum_scatter(
        jnp.einsum("kn,fn->kf", h_new, spectrogram, preferred_element_type=F32),
        "frame",
        scatter_dimension=0,
        tiled=True,
    ).T
    gram_local = jnp.einsum("kn,jn->kj", h_new, h_new, preferred_element_type=F32)
    gram = lax.psum(gram_local, "frame")
    own_cols = lax.dynamic_slice_in_dim(gram, lax.axis_index("frame") * note_cols, note_cols, 1)
    denom_w = jnp.dot(whole.astype(F32), own_cols, precision=lax.Precision.HIGHEST)
    temps = temps * numer_w / (denom_w + 1e-06)
    return (temps, acts)


def kernel(
    s_hbm, t_hbm, a_hbm, m_hbm, to_ref, ao_hbm,
    s_ref, t_ref, a_ref, m_ref, ao_ref, mt, wt, hbt, at, num, den, pnum, pden, hn, blk, out, xr, zr, gram,
    ls, ws, wr, ns, nr, ds, dr, xs, xrs, zs, zrs, gs, gr,
):
    own, bins = t_ref.shape
    notes, frames = a_ref.shape
    wide = bins + notes // 2
    half = notes // 2
    me = lax.axis_index("frame")
    c = lax.axis_index("freq")
    z, x = me // 2, me % 2
    across = z * 2 + 1 - x
    cp = 1 - c

    load_a = pltpu.make_async_copy(a_hbm, a_ref, ls.at[0])
    load_s = pltpu.make_async_copy(s_hbm, s_ref, ls.at[1])
    load_t = pltpu.make_async_copy(t_hbm, t_ref, ls.at[2])
    load_m = pltpu.make_async_copy(m_hbm, m_ref, ls.at[3])
    for load in (load_t, load_m, load_a, load_s):
        load.start()

    barrier = pltpu.get_barrier_semaphore()
    pl.semaphore_signal(barrier, inc=1, device_id={"frame": across}, device_id_type=MESH)
    pl.semaphore_signal(barrier, inc=1, device_id={"freq": cp}, device_id_type=MESH)

    @pl.when(z < 3)
    def _():
        pl.semaphore_signal(barrier, inc=1, device_id={"frame": me + 2}, device_id_type=MESH)

    @pl.when(z > 0)
    def _():
        pl.semaphore_signal(barrier, inc=1, device_id={"frame": me - 2}, device_id_type=MESH)

    load_t.wait()
    wt[me] = t_ref[...].astype(BF16)
    pl.semaphore_wait(barrier, 2 + (z + 2) // 3 + (5 - z) // 3)

    def shard(idx, way, part):
        to = {0: across, 1: me + 2, 2: me - 2}[way]
        rows = pl.ds(part * (own // 2), own // 2)
        return pltpu.make_async_remote_copy(
            wt.at[idx, rows], wt.at[idx, rows], ws.at[way, idx, part], wr.at[idx, part],
            device_id={"frame": to}, device_id_type=MESH,
        )

    def send(idx, way):
        for part in range(2):
            shard(idx, way, part).start()

    def arrive(idx):
        for part in range(2):
            shard(idx, 0, part).wait_recv()

    first, last = 1 - x, 7 - x

    def numer_copy(idx):
        return pltpu.make_async_remote_copy(
            num.at[idx], pnum.at[idx], ns.at[idx], nr.at[idx],
            device_id={"freq": cp}, device_id_type=MESH,
        )

    def numer(idx):
        num[idx] = jnp.dot(wt[idx], s_ref[...], preferred_element_type=F32)
        numer_copy(idx).start()

    send(me, 0)

    @pl.when(z < 3)
    def _():
        send(me, 1)

    @pl.when(z > 0)
    def _():
        send(me, 2)

    load_m.wait()
    flags = m_ref[...].astype(F32)
    mt[...] = jnp.concatenate([flags, flags], 0).T
    load_a.wait()
    for b in range(frames // BLOCK):
        cols = slice(b * BLOCK, (b + 1) * BLOCK)
        held = a_ref[:, cols] * mt[:, b : b + 1]
        hbt[cols, :] = held.T.astype(BF16)
    load_s.wait()

    def forward(s):
        low, high = me - 2 * s, me + 2 * s

        @pl.when(z >= s)
        def _():
            arrive(low)

            @pl.when(z < 3)
            def _():
                send(low, 1)

            shard(low, 0, 0).start()

            @pl.when(z > s)
            def _():
                shard(low, 0, 1).start()

        @pl.when(z + s < 4)
        def _():
            arrive(high)

            @pl.when(z > 0)
            def _():
                send(high, 2)

            shard(high, 0, 0).start()

            @pl.when(z + s < 3)
            def _():
                shard(high, 0, 1).start()

    def near(s):
        @pl.when(z >= s)
        def _():
            numer(me - 2 * s)

        @pl.when(z + s < 4)
        def _():
            numer(me + 2 * s)

    def far(s):
        @pl.when(z >= s)
        def _():
            idx = across - 2 * s
            shard(idx, 0, 0).wait_recv()

            @pl.when(jnp.logical_or(z > s, z == 3))
            def _():
                shard(idx, 0, 1).wait_recv()

            numer(idx)

        @pl.when(z + s < 4)
        def _():
            idx = across + 2 * s
            shard(idx, 0, 0).wait_recv()

            @pl.when(jnp.logical_or(z + s < 3, z == 0))
            def _():
                shard(idx, 0, 1).wait_recv()

            numer(idx)

    def along(up, down):
        @pl.when(z == up)
        def _():
            shard(first, 0, 1).wait_recv()
            shard(first, 1, 1).start()

        @pl.when(z == down)
        def _():
            shard(last, 0, 1).wait_recv()
            shard(last, 2, 1).start()

    forward(1)
    arrive(across)

    @pl.when(z == 0)
    def _():
        shard(first, 1, 1).start()

    @pl.when(z == 3)
    def _():
        shard(last, 2, 1).start()

    numer(me)
    numer(across)
    forward(2)
    near(1)
    along(1, 2)
    far(1)
    forward(3)
    near(2)
    along(2, 1)
    near(3)
    far(2)
    far(3)

    def store(j):
        rows = pl.ds(j * half, half)
        return pltpu.make_async_copy(ao_ref.at[rows], ao_hbm.at[rows], ls.at[4 + j])

    step = 256

    @pl.loop(0, bins // step)
    def _(j):
        cols = pl.ds(pl.multiple_of(j * step, step), step)
        w = wt[:, :, cols].reshape(notes, step)
        at[:, cols] = jnp.dot(hbt[...], w, preferred_element_type=F32).astype(BF16)

    def denom_copy(j):
        return pltpu.make_async_remote_copy(
            den.at[j], pden.at[j], ds.at[j], dr.at[j],
            device_id={"freq": cp}, device_id_type=MESH,
        )

    for j in range(2):
        w = wt[j * 4 : j * 4 + 4].reshape(half, bins)
        den[j] = lax.dot_general(w, at[...], NT, preferred_element_type=F32)
        denom_copy(j).start()

    for i in range(8):
        numer_copy(i).wait_recv()

    for j in range(2):
        denom_copy(j).wait_recv()
        rows = slice(j * half, (j + 1) * half)
        for b in range(frames // BLOCK):
            cols = slice(b * BLOCK, (b + 1) * BLOCK)
            allowed = mt[rows, b : b + 1]
            up = (num[j * 4 : j * 4 + 4, :, cols] + pnum[j * 4 : j * 4 + 4, :, cols]).reshape(half, BLOCK)
            under = den[j, :, cols] + pden[j, :, cols]
            new = allowed * (a_ref[rows, cols] * allowed) * up / (under + 1e-06)
            ao_ref[rows, cols] = new
            hn[rows, cols] = new.astype(BF16)
        store(j).start()

    order = [3 * (1 - z // 2), 0, 1 + z % 2, z]
    order[1] = 6 - order[0] - order[2] - z
    mine = pl.ds(pl.multiple_of(c * half, half), half)

    def partial(idx):
        h = hn[pl.ds(pl.multiple_of(idx * own, own), own), :]
        blk[idx, :, :bins] = lax.dot_general(h, s_ref[...], NT, preferred_element_type=F32)
        blk[idx, :, bins:] = lax.dot_general(h, hn[mine, :], NT, preferred_element_type=F32)

    def encode(idx):
        powers = []
        for cols in (slice(0, bins), slice(bins, wide)):
            v = blk[idx, :, cols]
            top = jnp.max(v, axis=1, keepdims=True)
            power = jnp.ceil(jnp.log2(jnp.maximum(top, 1e-30)))
            q = jnp.minimum(jnp.round(v * jnp.exp2(16.0 - power)) - 32768.0, 32767.0)
            out[idx, :, cols] = q.astype(jnp.int32).astype(jnp.int16)
            powers.append(jnp.broadcast_to(power, (own, BLOCK)))
        lane = lax.broadcasted_iota(jnp.int32, (own, BLOCK), 1)
        power = jnp.where(lane < BLOCK // 2, powers[0], powers[1])
        out[idx, :, wide:] = power.astype(jnp.int32).astype(jnp.int16)

    def add(idx, ref, pieces=(0, 1)):
        scale = jnp.exp2(ref[:, wide:].astype(jnp.int32).astype(F32) - 16.0)
        for piece in pieces:
            cols, col = ((slice(0, bins), 0), (slice(bins, wide), BLOCK - 1))[piece]
            v = ref[:, cols].astype(jnp.int32).astype(F32) + 32768.0
            blk[idx, :, cols] += v * scale[:, col : col + 1]

    def x_copy(d):
        return pltpu.make_async_remote_copy(
            out.at[2 * d + 1 - x], xr.at[d], xs.at[d], xrs.at[d],
            device_id={"frame": across}, device_id_type=MESH,
        )

    def z_copy(d, way):
        to = me + 2 if way else me - 2
        return pltpu.make_async_remote_copy(
            out.at[2 * d + x], zr.at[way, d], zs.at[d], zrs.at[way, d],
            device_id={"frame": to}, device_id_type=MESH,
        )

    for d in order:
        partial(2 * d + 1 - x)
        encode(2 * d + 1 - x)
        x_copy(d).start()

    for d in order[:3]:
        idx = 2 * d + x
        partial(idx)
        x_copy(d).wait_recv()
        add(idx, xr.at[d])

        @pl.when(d > z)
        def _():
            @pl.when(z > 0)
            def _():
                z_copy(d, 1).wait_recv()
                add(idx, zr.at[1, d])

            encode(idx)
            z_copy(d, 1).start()

        @pl.when(d < z)
        def _():
            @pl.when(z < 3)
            def _():
                z_copy(d, 0).wait_recv()
                add(idx, zr.at[0, d])

            encode(idx)
            z_copy(d, 0).start()

    partial(me)
    x_copy(z).wait_recv()
    @pl.when(z > 0)
    def _():
        z_copy(z, 1).wait_recv()

    @pl.when(z < 3)
    def _():
        z_copy(z, 0).wait_recv()

    def finish(pieces):
        add(me, xr.at[z], pieces)

        @pl.when(z > 0)
        def _():
            add(me, zr.at[1, z], pieces)

        @pl.when(z < 3)
        def _():
            add(me, zr.at[0, z], pieces)

    finish((1,))
    gram[c] = blk[me, :, bins:]
    share = pltpu.make_async_remote_copy(
        gram.at[c], gram.at[c], gs, gr, device_id={"freq": cp}, device_id_type=MESH
    )
    share.start()
    finish((0,))
    share.wait_recv()

    total = jnp.zeros((own, bins), F32)
    for j in range(2):
        g = gram[j]
        hi = g.astype(BF16)
        lo = (g - hi.astype(F32)).astype(BF16)
        w = wt[j * 4 : j * 4 + 4].reshape(half, bins)
        both = jnp.dot(jnp.concatenate([hi, lo], 0), w, preferred_element_type=F32)
        total = total + both[:own] + both[own:]
    to_ref[...] = t_ref[...] * blk[me, :, :bins] / (total + 1e-06)

    share.wait_send()
    for j in range(2):
        denom_copy(j).wait_send()
        store(j).wait()
    for i in range(8):
        numer_copy(i).wait_send()
    for d in range(4):
        x_copy(d).wait_send()
        shard(2 * d + x, 0, 0).wait_send()

        @pl.when(d == z if d in (0, 3) else d >= 0 * z)
        def _():
            shard(2 * d + x, 0, 1).wait_send()

        @pl.when(d != z)
        def _():
            z_copy(d, 0).wait_send()

        @pl.when(jnp.logical_and(d <= z, z < 3))
        def _():
            for part in range(2):
                shard(2 * d + x, 1, part).wait_send()

        @pl.when(jnp.logical_and(d >= z, z > 0))
        def _():
            for part in range(2):
                shard(2 * d + x, 2, part).wait_send()

    @pl.when(z < 3)
    def _():
        shard(first, 1, 1).wait_send()

    @pl.when(z > 0)
    def _():
        shard(last, 2, 1).wait_send()


def fused(spectrogram, templates, activations, score_mask):
    bins, own = templates.shape
    notes, frames = activations.shape
    half = notes // 2
    dma = pltpu.SemaphoreType.DMA
    wide = bins + half
    turned, acts = pl.pallas_call(
        kernel,
        out_shape=(
            jax.ShapeDtypeStruct((own, bins), F32),
            jax.ShapeDtypeStruct((notes, frames), F32),
        ),
        in_specs=[pl.BlockSpec(memory_space=pltpu.HBM)] * 4,
        out_specs=[pl.BlockSpec(memory_space=m) for m in (pltpu.VMEM, pltpu.HBM)],
        scratch_shapes=[
            pltpu.VMEM((bins, frames), BF16),
            pltpu.VMEM((own, bins), F32),
            pltpu.VMEM((notes, frames), F32),
            pltpu.VMEM((frames // BLOCK, notes), jnp.int32),
            pltpu.VMEM((notes, frames), F32),
            pltpu.VMEM((notes, 8), F32),
            pltpu.VMEM((8, own, bins), BF16),
            pltpu.VMEM((frames, notes), BF16),
            pltpu.VMEM((frames, bins), BF16),
            pltpu.VMEM((8, own, frames), F32),
            pltpu.VMEM((2, half, frames), F32),
            pltpu.VMEM((8, own, frames), F32),
            pltpu.VMEM((2, half, frames), F32),
            pltpu.VMEM((notes, frames), BF16),
            pltpu.VMEM((8, own, wide), F32),
            pltpu.VMEM((8, own, wide + BLOCK), jnp.int16),
            pltpu.VMEM((4, own, wide + BLOCK), jnp.int16),
            pltpu.VMEM((2, 4, own, wide + BLOCK), jnp.int16),
            pltpu.VMEM((2, own, half), F32),
            dma((6,)), dma((3, 8, 2)), dma((8, 2)), dma((8,)), dma((8,)), dma((2,)), dma((2,)),
            dma((4,)), dma((4,)), dma((4,)), dma((2, 4)), dma(()), dma(()),
        ],
        compiler_params=pltpu.CompilerParams(
            collective_id=0, has_side_effects=True, vmem_limit_bytes=53 * 1024 * 1024
        ),
    )(spectrogram, templates.T, activations, score_mask.T)
    return turned.T, acts


def solution(mesh):
    return jax.shard_map(
        fused if mesh.shape["frame"] == 8 else shards,
        mesh=mesh,
        in_specs=(
            P("freq", ("parts", "frame")),
            P(("parts", "freq"), "frame"),
            P(None, ("parts", "frame")),
            P(None, ("parts", "frame")),
        ),
        out_specs=(P(("parts", "freq"), "frame"), P(None, ("parts", "frame"))),
        check_vma=False,
    )
```
